256 devices in a mesh: grp: 4 (over x), blk: 64 (over z, y, core).
Axes of the slice: x: 4, y: 4, z: 8, core: 2. Of those that a mesh axis runs over, the one named last changes fastest.
Arguments:
- embeddings: bfloat16 [131072, 1024], P(('grp', 'blk')), may hold values from -6 to 6
- labels: int32 [131072], P(('grp', 'blk')), may hold values from 0 to 127, as said below
Outputs:
- best_match: float32 [131072], P(('grp', 'blk'))
The draws below stay inside these ranges and needn't reach their ends.
Inputs may be any that keep to these rules, and one draw needn't show every extreme that they name: `labels`: in each aligned block of 512 rows (the rows of one device), the rows whose cluster has owner index b (label // 2 == b) number either 0 or exactly 16, for every b; one owner index per index of grp may receive 16 rows from every one of that grp index's 64 blocks, so a device can receive up to 1024 rows; other owners receive fewer.
All inputs are finite; a program needn't handle non-finite values.
Results may differ from the reference program's by a relative error of at most 0.0014.
Values may be sent and summed in bfloat16 or wider, within the bound.
A program may use at most 64 MiB of HBM per device.

```python
import jax
import jax.numpy as jnp
from jax import lax

D = 1024
ROWS_PER_DEVICE = 512
CLUSTERS_PER_BLK = 2
CAP = 16
TOTAL = 131072
N_GRP = 4
N_BLK = 64


def draw_labels(key, part):
    key = jax.random.fold_in(key, 7)
    blocks = TOTAL // ROWS_PER_DEVICE
    groups = blocks // N_BLK
    favored_key, block_base = jax.random.split(key)
    favored_all = jax.random.randint(favored_key, (groups,), 0, N_BLK).astype(jnp.int32)
    favored_rows = jnp.repeat(favored_all, N_BLK)
    keys = jax.random.split(block_base, blocks)

    def one_block(block_key, favored):
        first_key, second_key, third_random_key = jax.random.split(block_key, 3)
        placed = jax.random.permutation(first_key, ROWS_PER_DEVICE)
        rank = placed // CAP
        others = jax.random.permutation(second_key, N_BLK - 1).astype(jnp.int32)
        others = others + (others >= favored).astype(jnp.int32)
        owners = jnp.concatenate([favored[None], others])
        target_index = owners[rank]
        local_rows = jax.random.randint(third_random_key, (ROWS_PER_DEVICE,), 0, CLUSTERS_PER_BLK)
        return target_index * CLUSTERS_PER_BLK + local_rows
    return jax.vmap(one_block)(keys, favored_rows).reshape(-1).astype(jnp.int32)


def shard_levels(key, shape, pieces, least, largest):
    loudness, own = 1.0, jax.random.fold_in(key, 6)
    for dim, parts in pieces:
        steps = jnp.exp(jax.random.uniform(jax.random.fold_in(own, dim), (parts,), jnp.float32, least / len(pieces), largest / len(pieces)))
        loudness = loudness * jnp.repeat(steps, shape[dim] // parts).reshape([-1 if axis == dim else 1 for axis in range(len(shape))])
    return loudness


def gaussian(own_key, dims, scale, reach, cuts=(), held_as=jnp.bfloat16):
    array = scale * jax.random.normal(own_key, dims, jnp.float32)
    if cuts:
        array = array * shard_levels(own_key, dims, cuts, -0.22, 0.18)
    return jnp.clip(array, -reach, reach).astype(held_as)


def setup_inputs(seed: int = 0) -> dict:
    streams_of = jax.random.split(jax.random.key(seed), 3)
    return {
        "embeddings": gaussian(streams_of[0], (TOTAL, D), 1.0, 6.0, ((0, 256),)),
        "labels": draw_labels(jax.random.fold_in(streams_of[2], 71), 0),
    }


def reference(embeddings, labels):
    values = embeddings.astype(jnp.float32)
    unit = (values * lax.rsqrt(lax.optimization_barrier(jnp.sum(values * values, axis=1, keepdims=True)) + 1e-06)).astype(jnp.bfloat16)
    owner_index = labels // CLUSTERS_PER_BLK
    width = 2 * ROWS_PER_DEVICE * N_GRP
    block = min(512, width)

    def per_owner(index):
        order = jnp.argsort((owner_index != index).astype(jnp.int32), stable=True)[:width]
        counted = jnp.sum((owner_index == index).astype(jnp.int32))
        valid = jnp.arange(width, dtype=jnp.int32) < counted
        rows = unit[order]
        marks = jnp.where(valid, labels[order], -1)

        def per_block(first):
            part = lax.dynamic_slice_in_dim(rows, first, block, 0)
            part_marks = lax.dynamic_slice_in_dim(marks, first, block, 0)
            scores = jnp.dot(part, rows.T, preferred_element_type=jnp.float32)
            here = first + jnp.arange(block, dtype=jnp.int32)
            there = jnp.arange(width, dtype=jnp.int32)
            keep = (part_marks[:, None] == marks[None, :]) & (part_marks[:, None] >= 0) & (here[:, None] != there[None, :])
            return lax.optimization_barrier(jnp.max(jnp.where(keep, scores, -1.0), axis=1))
        starts = jnp.arange(0, width, block, dtype=jnp.int32)
        found = lax.map(per_block, starts).reshape(-1)
        target_index = jnp.where(valid, order, TOTAL).astype(jnp.int32)
        return (target_index, found)
    targets, founds = lax.map(per_owner, jnp.arange(N_BLK, dtype=jnp.int32))
    result = jnp.full((TOTAL,), -1.0, jnp.float32)
    return result.at[targets.reshape(-1)].set(founds.reshape(-1), mode='drop')
```

```python
import functools

import jax
import jax.numpy as jnp
from jax import lax
from jax.experimental import pallas as pl
from jax.experimental.pallas import tpu as pltpu
from jax.sharding import PartitionSpec as P

MESH = pl.DeviceIdType.MESH
F32 = jnp.float32
BF16 = jnp.bfloat16

NX, NY, NZ = 4, 4, 8
CAP = 16
STEPS = 8
GROUP = 256
D = 1024


def place():
    x, b = lax.axis_index("grp"), lax.axis_index("blk")
    return x, lax.rem(lax.div(b, 2), NY), lax.div(b, 2 * NY), lax.rem(b, 2)


def device(x, y, z, c):
    return (x, z * (2 * NY) + y * 2 + c)


def z_offset(t):
    return jnp.where(lax.rem(t, 2) == 1, lax.div(t + 1, 2), lax.rem(NZ - lax.div(t, 2), NZ))


def remote(src, dst, send, recv, where):
    return pltpu.make_async_remote_copy(
        src_ref=src, dst_ref=dst, send_sem=send, recv_sem=recv, device_id=where, device_id_type=MESH
    )


def arrived(ref, sem):
    pltpu.make_async_copy(ref, ref, sem).wait()


def iota(shape, dim):
    return lax.broadcasted_iota(jnp.int32, shape, dim)


def kernel(
    emb_hbm, labels, out, emb, src, marks, rows, row_marks_in, row_marks, col_marks, best, result, results, back, backs,
    load_sem, send_sem, recv_sem, mark_send_sem, mark_recv_sem, pair_send_sem, pair_recv_sem, pair_mark_send_sem,
    pair_mark_recv_sem, result_send_sem, result_recv_sem, back_send_sem, back_recv_sem,
):
    x, y, z, c = place()
    parity = lax.rem(x + y + z, 2)
    is_owner = parity == 0
    pair = device(x, y, z, 1 - c)

    load = pltpu.make_async_copy(emb_hbm, emb, load_sem)
    load.start()
    barrier = pltpu.get_barrier_semaphore()

    @pl.when(is_owner)
    def _():
        def greet(n, carry):
            to = device(
                lax.rem(x + lax.rem(n, NX), NX), lax.rem(y + lax.rem(lax.div(n, NX), NY), NY),
                lax.rem(z + lax.div(n, NX * NY), NZ), c,
            )
            pl.semaphore_signal(barrier, inc=1, device_id=to, device_id_type=MESH)
            return carry

        lax.fori_loop(1, NX * NY * NZ, greet, 0)
        pl.semaphore_signal(barrier, inc=1, device_id=pair, device_id_type=MESH)

    held = emb.shape[0]
    owner_of = lax.div(labels[...], 2)
    chosen = (iota((64, held), 0) == owner_of).astype(F32)
    before = (iota((held, held), 0) < iota((held, held), 1)).astype(F32).astype(BF16)
    count = jnp.dot(chosen.astype(BF16), before, preferred_element_type=F32)
    position = jnp.sum(chosen * count, axis=0, keepdims=True).astype(jnp.int32)
    flat = owner_of * CAP + position
    at_lane = jnp.where(lax.rem(iota((128, held), 0), CAP) == position, 1 + lax.rem(labels[...], 2), 0).astype(F32)
    marks[...] = lax.dot_general(
        chosen.astype(BF16), at_lane.astype(BF16), (((1,), (1,)), ((), ())), preferred_element_type=F32
    )

    load.wait()

    def normalise(n, carry):
        part = pl.ds(n * 64, 64)
        values = emb[part, :].astype(F32)
        scale = lax.rsqrt(jnp.sum(values * values, axis=1, keepdims=True) + 1e-06)
        emb[part, :] = (values * scale).astype(BF16)
        return carry

    lax.fori_loop(0, held // 64, normalise, 0)

    def targets(i):
        out = []
        for j in range(8):
            dz = z_offset(lax.rem(i + j, 8))
            dy, h = j // 2, j % 2
            q = lax.rem(parity + dy + dz, 2)
            to = (lax.rem(x + 2 * h + q, NX), lax.rem(y + dy, NY), lax.rem(z + dz, NZ))
            out.append((to[2] * 8 + to[1] * 2 + lax.div(to[0], 2), q, device(*to, c)))
        return out

    def pack(i, to):
        chosen_rows = jnp.concatenate(
            [jnp.where(iota((CAP, held), 0) == flat - b * CAP, 1.0, 0.0) for b, _, _ in to], axis=0
        ).astype(BF16)
        src[pl.ds(pl.multiple_of(i * 128, 128), 128), :] = jnp.dot(
            chosen_rows, emb[...], preferred_element_type=F32
        ).astype(BF16)

    def copies(i, j, b, q):
        slot = 2 * j + q
        return (
            src.at[pl.ds(pl.multiple_of(i * 128 + j * CAP, CAP), CAP)],
            rows.at[i, pl.ds(pl.multiple_of(slot * CAP, CAP), CAP)],
            marks.at[pl.ds(b, 1)],
            row_marks_in.at[i, pl.ds(slot, 1)],
        )

    def send(i, j, b, q, where):
        s, d, ms, md = copies(i, j, b, q)
        remote(s, d, send_sem, recv_sem.at[i], where).start()
        remote(ms, md, mark_send_sem, mark_recv_sem.at[i], where).start()

    first = targets(0)
    pack(0, first)
    pl.semaphore_wait(barrier, 64)
    for j in range(8):
        b, q, where = first[j]
        if j == 0:

            @pl.when(is_owner)
            def _():
                s, d, ms, md = copies(0, 0, b, 0)
                pltpu.make_async_copy(s, d, recv_sem.at[0]).start()
                pltpu.make_async_copy(ms, md, mark_recv_sem.at[0]).start()

            @pl.when(jnp.logical_not(is_owner))
            def _():
                send(0, 0, b, q, where)
        else:
            send(0, j, b, q, where)

    def step(i, carry):
        to = targets(i)
        pack(i, to)
        for j in range(8):
            send(i, j, *to[j])
        return carry

    lax.fori_loop(1, STEPS, step, 0)

    @pl.when(is_owner)
    def _():
        best[...] = jnp.full(best.shape, -1.0, F32)
        lane = iota((16, 128), 1)
        mine = lax.div(lane, CAP) == lax.rem(iota((16, 128), 0), 8)
        diagonal = lax.rem(iota((16, CAP, 128), 2), 128) == iota((16, CAP, 128), 1)

        def spread(i, half):
            m = row_marks_in[i, pl.ds(half * 16, 16), :]
            column = jnp.sum(jnp.where(diagonal, m.reshape(16, 1, 128), 0.0), axis=2, keepdims=True)
            row_marks[i, pl.ds(half * GROUP, GROUP), :] = jnp.broadcast_to(column, (16, CAP, 128)).reshape(GROUP, 128)
            return m

        def tile(k, first_row, size, col, diag=False):
            left = rows[k, pl.ds(first_row, size), :]
            right = rows[col, pl.ds(0, GROUP), :]
            sim = lax.dot_general(left, right, (((1,), (1,)), ((), ())), preferred_element_type=F32)
            m = row_marks[k, pl.ds(first_row, size), :]
            keep = jnp.concatenate([m, m], axis=1) == col_marks[col, 0:1, :]
            if diag:
                keep = keep & (iota((size, GROUP), 0) != iota((size, GROUP), 1))
            sim = jnp.where(keep, sim, -1.0)
            best[col] = jnp.maximum(best[col], jnp.max(sim.reshape(size // 8, 8, GROUP), axis=0))

        def group(i, carry):
            arrived(rows.at[i, pl.ds(0, GROUP)], recv_sem.at[i])
            arrived(row_marks_in.at[i, pl.ds(0, 16)], mark_recv_sem.at[i])
            remote(
                rows.at[i, pl.ds(0, GROUP)], rows.at[i, pl.ds(GROUP, GROUP)], pair_send_sem, pair_recv_sem.at[i], pair
            ).start()
            remote(
                row_marks_in.at[i, pl.ds(0, 16)], row_marks_in.at[i, pl.ds(16, 16)], pair_mark_send_sem,
                pair_mark_recv_sem.at[i], pair,
            ).start()
            m = spread(i, 0)
            lanes = jnp.sum(jnp.where(mine, m, 0.0).reshape(2, 8, 128), axis=1)
            col_marks[i] = jnp.broadcast_to(jnp.concatenate([lanes[0:1], lanes[1:2]], axis=1), (8, GROUP))
            tile(i, 0, GROUP, i, diag=True)

            def earlier(k, carry):
                tile(k, 0, 2 * GROUP, i)
                tile(i, 0, GROUP, k)
                return carry

            lax.fori_loop(0, i, earlier, 0)
            arrived(rows.at[i, pl.ds(GROUP, GROUP)], pair_recv_sem.at[i])
            arrived(row_marks_in.at[i, pl.ds(16, 16)], pair_mark_recv_sem.at[i])
            spread(i, 1)

            def all_columns(k, carry):
                tile(i, GROUP, GROUP, k)
                return carry

            lax.fori_loop(0, i + 1, all_columns, 0)
            return carry

        lax.fori_loop(0, STEPS, group, 0)
        for i in range(STEPS):
            top = jnp.max(best[i], axis=0, keepdims=True)
            result[pl.ds(2 * i, 1), :] = top[:, 0:128]
            result[pl.ds(2 * i + 1, 1), :] = top[:, 128:256]
        me = y * 2 + lax.div(x, 2)
        pltpu.make_async_copy(result, results.at[me], result_recv_sem).start()
        for n in range(1, NX * NY):
            where = device(lax.rem(x + n % NX, NX), lax.rem(y + n // NX, NY), z, c)
            remote(result, results.at[me], result_send_sem, result_recv_sem, where).start()

    arrived(results, result_recv_sem)
    for o in range(8):
        oy = o // 2
        ox = 2 * (o % 2) + lax.rem(oy + z, 2)
        dx = lax.rem(ox - x + NX, NX)
        j = lax.rem(oy - y + NY, NY) * 2 + lax.div(dx, 2)

        def turn(t, carry):
            i = lax.rem(t - j + 8, 8)
            back[t, pl.ds(o, 1), :] = results[o, pl.ds(2 * i + lax.div(j, 4), 1), :]
            return carry

        lax.fori_loop(0, NZ, turn, 0)
    pltpu.make_async_copy(back.at[0], backs.at[z], back_recv_sem).start()
    for t in range(1, NZ):
        dz = (t + 1) // 2 if t % 2 else (NZ - t // 2) % NZ
        where = device(x, y, lax.rem(z - dz + NZ, NZ), c)
        remote(back.at[t], backs.at[z], back_send_sem, back_recv_sem, where).start()
    arrived(backs, back_recv_sem)

    b = iota((64, 128), 0)
    oz, oy = lax.div(b, 8), lax.rem(lax.div(b, 2), NY)
    ox = 2 * lax.rem(b, 2) + lax.rem(oy + oz, 2)
    dx = lax.rem(ox - x + NX, NX)
    j = lax.rem(oy - y + NY, NY) * 2 + lax.div(dx, 2)
    ours = lax.div(iota((64, 128), 1), CAP) == lax.rem(j, 4) * 2 + lax.rem(dx, 2)
    left = jnp.where(ours, backs[...].reshape(64, 128), 0.0)
    left = jnp.concatenate([left, jnp.zeros((64, 128), F32)], axis=0).T
    owner_of = lax.div(labels[...], 2)
    chosen = (iota((128, held), 0) == owner_of).astype(F32).astype(BF16)
    spread_out = jnp.zeros((128, held), F32)
    for _ in range(3):
        term = left.astype(BF16)
        spread_out = spread_out + jnp.dot(term, chosen, preferred_element_type=F32)
        left = left - term.astype(F32)
    hit = lax.rem(iota((128, held), 0), CAP) == position
    out[...] = jnp.sum(jnp.where(hit, spread_out, 0.0), axis=0, keepdims=True)

    @pl.when(is_owner)
    def _():
        arrived(src.at[pl.ds(0, 63 * CAP)], send_sem)
        arrived(marks.at[pl.ds(0, 63)], mark_send_sem)
        arrived(rows.at[pl.ds(0, 4)], pair_send_sem)
        arrived(row_marks_in.at[pl.ds(0, 4)], pair_mark_send_sem)

        arrived(row_marks.at[0, pl.ds(0, 15 * 16)], result_send_sem)

    @pl.when(jnp.logical_not(is_owner))
    def _():
        arrived(src, send_sem)
        arrived(marks, mark_send_sem)

    arrived(back.at[pl.ds(1, 7)], back_send_sem)


def shards(embeddings, labels):
    held = embeddings.shape[0]
    dma = pltpu.SemaphoreType.DMA
    best = pl.pallas_call(
        kernel,
        out_shape=jax.ShapeDtypeStruct((1, held), F32),
        in_specs=[pl.BlockSpec(memory_space=pl.ANY), pl.BlockSpec(memory_space=pltpu.VMEM)],
        out_specs=pl.BlockSpec(memory_space=pltpu.VMEM),
        scratch_shapes=[
            pltpu.VMEM((held, D), BF16),
            pltpu.VMEM((STEPS * 8 * CAP, D), BF16),
            pltpu.VMEM((64, 128), F32),
            pltpu.VMEM((STEPS, 2 * GROUP, D), BF16),
            pltpu.VMEM((STEPS, 32, 128), F32),
            pltpu.VMEM((STEPS, 2 * GROUP, 128), F32),
            pltpu.VMEM((STEPS, 8, GROUP), F32),
            pltpu.VMEM((STEPS, 8, GROUP), F32),
            pltpu.VMEM((16, 128), F32),
            pltpu.VMEM((8, 16, 128), F32),
            pltpu.VMEM((NZ, 8, 128), F32),
            pltpu.VMEM((NZ, 8, 128), F32),
            dma, dma, dma((STEPS,)), dma, dma((STEPS,)), dma, dma((STEPS,)), dma, dma((STEPS,)), dma, dma, dma, dma,
        ],
        compiler_params=pltpu.CompilerParams(
            collective_id=0, has_side_effects=True, vmem_limit_bytes=48 * 2**20
        ),
    )(embeddings, labels.reshape(1, held))
    return best.reshape(held)


def solution(mesh):
    in_specs = (P(("grp", "blk"), None), P(("grp", "blk")))
    out_specs = P(("grp", "blk"))
    return jax.shard_map(shards, mesh=mesh, in_specs=in_specs, out_specs=out_specs, check_vma=False)
```

```python
import functools

import jax
import jax.numpy as jnp
from jax import lax
from jax.experimental import pallas as pl
from jax.experimental.pallas import tpu as pltpu
from jax.sharding import PartitionSpec as P

MESH = pl.DeviceIdType.MESH
F32 = jnp.float32
BF16 = jnp.bfloat16

NX, NY, NZ = 4, 4, 8
CAP = 16
STEPS = 8
GROUP = 256
D = 1024
UNROLLED = 2
LOAD = 128


def place():
    x, b = lax.axis_index("grp"), lax.axis_index("blk")
    return x, lax.rem(lax.div(b, 2), NY), lax.div(b, 2 * NY), lax.rem(b, 2)


def device(x, y, z, c):
    return (x, z * (2 * NY) + y * 2 + c)


def z_offset(t):
    return jnp.where(lax.rem(t, 2) == 1, lax.div(t + 1, 2), lax.rem(NZ - lax.div(t, 2), NZ))


def remote(src, dst, send, recv, where):
    return pltpu.make_async_remote_copy(
        src_ref=src, dst_ref=dst, send_sem=send, recv_sem=recv, device_id=where, device_id_type=MESH
    )


def arrived(ref, sem):
    pltpu.make_async_copy(ref, ref, sem).wait()


def iota(shape, dim):
    return lax.broadcasted_iota(jnp.int32, shape, dim)


def kernel(
    emb_hbm, labels_hbm, out, emb, labels, src, marks, rows, row_marks_in, row_marks, col_marks, best, result, results, back, backs,
    load_sem, label_sem, send_sem, recv_sem, mark_send_sem, mark_recv_sem, pair_send_sem, pair_recv_sem, pair_mark_send_sem,
    pair_mark_recv_sem, result_send_sem, result_recv_sem, back_send_sem, back_recv_sem,
):
    x, y, z, c = place()
    parity = lax.rem(x + y + z, 2)
    is_owner = parity == 0
    pair = device(x, y, z, 1 - c)

    label_load = pltpu.make_async_copy(labels_hbm, labels, label_sem)
    label_load.start()

    def load(n):
        part = pl.ds(n * LOAD, LOAD)
        return pltpu.make_async_copy(emb_hbm.at[part], emb.at[part], load_sem.at[n])

    for n in range(emb.shape[0] // LOAD):
        load(n).start()
    barrier = pltpu.get_barrier_semaphore()

    @pl.when(is_owner)
    def _():
        plane = [device(lax.rem(x + n % NX, NX), lax.rem(y + n // NX, NY), 0, c) for n in range(NX * NY)]

        def greet(n, carry):
            ahead = lax.rem(z + n, NZ) * (2 * NY)
            for gx, gb in plane:
                pl.semaphore_signal(barrier, inc=1, device_id=(gx, gb + ahead), device_id_type=MESH)
            return carry

        lax.fori_loop(1, NZ, greet, 0)
        for gx, gb in plane[1:]:
            pl.semaphore_signal(barrier, inc=1, device_id=(gx, gb + z * (2 * NY)), device_id_type=MESH)
        pl.semaphore_signal(barrier, inc=1, device_id=pair, device_id_type=MESH)

    held = emb.shape[0]
    before = (iota((held, held), 0) < iota((held, held), 1)).astype(F32).astype(BF16)
    label_load.wait()
    owner_of = lax.div(labels[...], 2)
    chosen = (iota((64, held), 0) == owner_of).astype(F32)
    count = jnp.dot(chosen.astype(BF16), before, preferred_element_type=F32)
    position = jnp.sum(chosen * count, axis=0, keepdims=True).astype(jnp.int32)
    flat = owner_of * CAP + position
    at_lane = jnp.where(lax.rem(iota((128, held), 0), CAP) == position, 1 + lax.rem(labels[...], 2), 0).astype(F32)
    marks[...] = lax.dot_general(
        chosen.astype(BF16), at_lane.astype(BF16), (((1,), (1,)), ((), ())), preferred_element_type=F32
    )

    for n in range(held // LOAD):
        load(n).wait()
        part = pl.ds(n * LOAD, LOAD)
        values = emb[part, :].astype(F32)
        scale = lax.rsqrt(jnp.sum(values * values, axis=1, keepdims=True) + 1e-06)
        emb[part, :] = (values * scale).astype(BF16)

    def targets(i):
        out = []
        for j in range(8):
            dz = z_offset(lax.rem(i + j, 8))
            dy, h = j // 2, j % 2
            q = lax.rem(parity + dy + dz, 2)
            to = (lax.rem(x + 2 * h + q, NX), lax.rem(y + dy, NY), lax.rem(z + dz, NZ))
            out.append((to[2] * 8 + to[1] * 2 + lax.div(to[0], 2), q, device(*to, c)))
        return out

    def pack(i, to):
        chosen_rows = jnp.concatenate(
            [jnp.where(iota((CAP, held), 0) == flat - b * CAP, 1.0, 0.0) for b, _, _ in to], axis=0
        ).astype(BF16)
        src[pl.ds(pl.multiple_of(i * 128, 128), 128), :] = jnp.dot(
            chosen_rows, emb[...], preferred_element_type=F32
        ).astype(BF16)

    def copies(i, j, b, q):
        slot = 2 * j + q
        return (
            src.at[pl.ds(pl.multiple_of(i * 128 + j * CAP, CAP), CAP)],
            rows.at[i, pl.ds(pl.multiple_of(slot * CAP, CAP), CAP)],
            marks.at[pl.ds(b, 1)],
            row_marks_in.at[i, pl.ds(slot, 1)],
        )

    def send(i, j, b, q, where):
        s, d, ms, md = copies(i, j, b, q)
        remote(s, d, send_sem, recv_sem.at[i], where).start()
        remote(ms, md, mark_send_sem, mark_recv_sem.at[i], where).start()

    first = targets(0)
    pack(0, first)
    pl.semaphore_wait(barrier, 64)
    for j in range(8):
        b, q, where = first[j]
        if j == 0:

            @pl.when(is_owner)
            def _():
                s, d, ms, md = copies(0, 0, b, 0)
                pltpu.make_async_copy(s, d, recv_sem.at[0]).start()
                pltpu.make_async_copy(ms, md, mark_recv_sem.at[0]).start()

            @pl.when(jnp.logical_not(is_owner))
            def _():
                send(0, 0, b, q, where)
        else:
            send(0, j, b, q, where)

    def step(i, carry):
        to = targets(i)
        pack(i, to)
        for j in range(8):
            send(i, j, *to[j])
        return carry

    lax.fori_loop(1, STEPS, step, 0)

    @pl.when(is_owner)
    def _():
        lane = iota((16, 128), 1)
        mine = lax.div(lane, CAP) == lax.rem(iota((16, 128), 0), 8)
        diagonal = lax.rem(iota((16, CAP, 128), 2), 128) == iota((16, CAP, 128), 1)

        def spread(i, half):
            m = row_marks_in[i, pl.ds(half * 16, 16), :]
            column = jnp.sum(jnp.where(diagonal, m.reshape(16, 1, 128), 0.0), axis=2, keepdims=True)
            row_marks[i, pl.ds(half * GROUP, GROUP), :] = jnp.broadcast_to(column, (16, CAP, 128)).reshape(GROUP, 128)
            return m

        def tile(k, first_row, size, col, diag=False):
            left = rows[k, pl.ds(first_row, size), :]
            right = rows[col, pl.ds(0, GROUP), :]
            sim = lax.dot_general(left, right, (((1,), (1,)), ((), ())), preferred_element_type=F32)
            m = row_marks[k, pl.ds(first_row, size), :]
            keep = jnp.concatenate([m, m], axis=1) == col_marks[col, 0:1, :]
            if diag:
                keep = keep & (iota((size, GROUP), 0) != iota((size, GROUP), 1))
            return jnp.max(jnp.where(keep, sim, -1.0).reshape(size // 8, 8, GROUP), axis=0)

        def loop(n, body, init):
            if isinstance(n, int):
                for k in range(n):
                    init = body(k, init)
                return init
            return lax.fori_loop(0, n, body, init)

        def group(i, carry):
            arrived(rows.at[i, pl.ds(0, GROUP)], recv_sem.at[i])
            arrived(row_marks_in.at[i, pl.ds(0, 16)], mark_recv_sem.at[i])
            remote(
                rows.at[i, pl.ds(0, GROUP)], rows.at[i, pl.ds(GROUP, GROUP)], pair_send_sem, pair_recv_sem.at[i], pair
            ).start()
            remote(
                row_marks_in.at[i, pl.ds(0, 16)], row_marks_in.at[i, pl.ds(16, 16)], pair_mark_send_sem,
                pair_mark_recv_sem.at[i], pair,
            ).start()
            m = spread(i, 0)
            lanes = jnp.sum(jnp.where(mine, m, 0.0).reshape(2, 8, 128), axis=1)
            col_marks[i] = jnp.broadcast_to(jnp.concatenate([lanes[0:1], lanes[1:2]], axis=1), (8, GROUP))

            def earlier(k, top):
                best[k] = jnp.maximum(best[k], tile(i, 0, GROUP, k))
                return jnp.maximum(top, tile(k, 0, 2 * GROUP, i))

            top = loop(i, earlier, tile(i, 0, GROUP, i, diag=True))
            arrived(rows.at[i, pl.ds(GROUP, GROUP)], pair_recv_sem.at[i])
            arrived(row_marks_in.at[i, pl.ds(16, 16)], pair_mark_recv_sem.at[i])
            spread(i, 1)
            best[i] = jnp.maximum(top, tile(i, GROUP, GROUP, i))

            def others(k, carry):
                best[k] = jnp.maximum(best[k], tile(i, GROUP, GROUP, k))
                return carry

            loop(i, others, 0)
            return carry

        lax.fori_loop(0, STEPS - UNROLLED, group, 0)
        for i in range(STEPS - UNROLLED, STEPS):
            group(i, 0)
        for i in range(STEPS):
            top = jnp.max(best[i], axis=0, keepdims=True)
            result[pl.ds(2 * i, 1), :] = top[:, 0:128]
            result[pl.ds(2 * i + 1, 1), :] = top[:, 128:256]
        me = y * 2 + lax.div(x, 2)
        pltpu.make_async_copy(result, results.at[me], result_recv_sem).start()
        for n in range(1, NX * NY):
            where = device(lax.rem(x + n % NX, NX), lax.rem(y + n // NX, NY), z, c)
            remote(result, results.at[me], result_send_sem, result_recv_sem, where).start()

    arrived(results, result_recv_sem)
    for o in range(8):
        oy = o // 2
        ox = 2 * (o % 2) + lax.rem(oy + z, 2)
        dx = lax.rem(ox - x + NX, NX)
        j = lax.rem(oy - y + NY, NY) * 2 + lax.div(dx, 2)

        def turn(t, carry):
            i = lax.rem(t - j + 8, 8)
            back[t, pl.ds(o, 1), :] = results[o, pl.ds(2 * i + lax.div(j, 4), 1), :]
            return carry

        lax.fori_loop(0, NZ, turn, 0)
    pltpu.make_async_copy(back.at[0], backs.at[z], back_recv_sem).start()
    for t in range(1, NZ):
        dz = (t + 1) // 2 if t % 2 else (NZ - t // 2) % NZ
        where = device(x, y, lax.rem(z - dz + NZ, NZ), c)
        remote(back.at[t], backs.at[z], back_send_sem, back_recv_sem, where).start()
    arrived(backs, back_recv_sem)

    b = iota((64, 128), 0)
    oz, oy = lax.div(b, 8), lax.rem(lax.div(b, 2), NY)
    ox = 2 * lax.rem(b, 2) + lax.rem(oy + oz, 2)
    dx = lax.rem(ox - x + NX, NX)
    j = lax.rem(oy - y + NY, NY) * 2 + lax.div(dx, 2)
    ours = lax.div(iota((64, 128), 1), CAP) == lax.rem(j, 4) * 2 + lax.rem(dx, 2)
    left = jnp.where(ours, backs[...].reshape(64, 128), 0.0)
    left = jnp.concatenate([left, jnp.zeros((64, 128), F32)], axis=0).T
    owner_of = lax.div(labels[...], 2)
    chosen = (iota((128, held), 0) == owner_of).astype(F32).astype(BF16)
    spread_out = jnp.zeros((128, held), F32)
    for _ in range(3):
        term = left.astype(BF16)
        spread_out = spread_out + jnp.dot(term, chosen, preferred_element_type=F32)
        left = left - term.astype(F32)
    hit = lax.rem(iota((128, held), 0), CAP) == position
    out[...] = jnp.sum(jnp.where(hit, spread_out, 0.0), axis=0, keepdims=True)

    @pl.when(is_owner)
    def _():
        arrived(src.at[pl.ds(0, 63 * CAP)], send_sem)
        arrived(marks.at[pl.ds(0, 63)], mark_send_sem)
        arrived(rows.at[pl.ds(0, 4)], pair_send_sem)
        arrived(row_marks_in.at[pl.ds(0, 4)], pair_mark_send_sem)

        arrived(row_marks.at[0, pl.ds(0, 15 * 16)], result_send_sem)

    @pl.when(jnp.logical_not(is_owner))
    def _():
        arrived(src, send_sem)
        arrived(marks, mark_send_sem)

    arrived(back.at[pl.ds(1, 7)], back_send_sem)


def shards(embeddings, labels):
    held = embeddings.shape[0]
    dma = pltpu.SemaphoreType.DMA
    best = pl.pallas_call(
        kernel,
        out_shape=jax.ShapeDtypeStruct((1, held), F32),
        in_specs=[pl.BlockSpec(memory_space=pl.ANY)] * 2,
        out_specs=pl.BlockSpec(memory_space=pltpu.VMEM),
        scratch_shapes=[
            pltpu.VMEM((held, D), BF16),
            pltpu.VMEM((1, held), jnp.int32),
            pltpu.VMEM((STEPS * 8 * CAP, D), BF16),
            pltpu.VMEM((64, 128), F32),
            pltpu.VMEM((STEPS, 2 * GROUP, D), BF16),
            pltpu.VMEM((STEPS, 32, 128), F32),
            pltpu.VMEM((STEPS, 2 * GROUP, 128), F32),
            pltpu.VMEM((STEPS, 8, GROUP), F32),
            pltpu.VMEM((STEPS, 8, GROUP), F32),
            pltpu.VMEM((16, 128), F32),
            pltpu.VMEM((8, 16, 128), F32),
            pltpu.VMEM((NZ, 8, 128), F32),
            pltpu.VMEM((NZ, 8, 128), F32),
            dma((held // LOAD,)), dma, dma, dma((STEPS,)), dma, dma((STEPS,)), dma, dma((STEPS,)), dma, dma((STEPS,)), dma, dma, dma, dma,
        ],
        compiler_params=pltpu.CompilerParams(
            collective_id=0, has_side_effects=True, vmem_limit_bytes=62 * 2**20
        ),
    )(embeddings, labels.reshape(1, held))
    return best.reshape(held)


def solution(mesh):
    in_specs = (P(("grp", "blk"), None), P(("grp", "blk")))
    out_specs = P(("grp", "blk"))
    return jax.shard_map(shards, mesh=mesh, in_specs=in_specs, out_specs=out_specs, check_vma=False)
```

```python
import functools

import jax
import jax.numpy as jnp
from jax import lax
from jax.experimental import pallas as pl
from jax.experimental.pallas import tpu as pltpu
from jax.sharding import PartitionSpec as P

MESH = pl.DeviceIdType.MESH
F32 = jnp.float32
BF16 = jnp.bfloat16

NX, NY, NZ = 4, 4, 8
CAP = 16
STEPS = 8
GROUP = 256
D = 1024
UNROLLED = 2
LOAD = 128


def place():
    x, b = lax.axis_index("grp"), lax.axis_index("blk")
    return x, lax.rem(lax.div(b, 2), NY), lax.div(b, 2 * NY), lax.rem(b, 2)


def device(x, y, z, c):
    return (x, z * (2 * NY) + y * 2 + c)


def z_offset(t):
    return jnp.where(lax.rem(t, 2) == 1, lax.div(t + 1, 2), lax.rem(NZ - lax.div(t, 2), NZ))


def remote(src, dst, send, recv, where):
    return pltpu.make_async_remote_copy(
        src_ref=src, dst_ref=dst, send_sem=send, recv_sem=recv, device_id=where, device_id_type=MESH
    )


def arrived(ref, sem):
    pltpu.make_async_copy(ref, ref, sem).wait()


def iota(shape, dim):
    return lax.broadcasted_iota(jnp.int32, shape, dim)


def kernel(
    emb_hbm, labels_hbm, out, emb, labels, src, marks, rows, row_marks_in, row_marks, col_marks, best, result, results,
    load_sem, label_sem, send_sem, recv_sem, mark_send_sem, mark_recv_sem, pair_send_sem, pair_recv_sem, pair_mark_send_sem,
    pair_mark_recv_sem, result_send_sem, result_recv_sem,
):
    x, y, z, c = place()
    parity = lax.rem(x + y + z, 2)
    is_owner = parity == 0
    pair = device(x, y, z, 1 - c)

    label_load = pltpu.make_async_copy(labels_hbm, labels, label_sem)
    label_load.start()

    def load(n):
        part = pl.ds(n * LOAD, LOAD)
        return pltpu.make_async_copy(emb_hbm.at[part], emb.at[part], load_sem.at[n])

    for n in range(emb.shape[0] // LOAD):
        load(n).start()
    barrier = pltpu.get_barrier_semaphore()

    @pl.when(is_owner)
    def _():
        plane = [device(lax.rem(x + n % NX, NX), lax.rem(y + n // NX, NY), 0, c) for n in range(NX * NY)]

        def greet(n, carry):
            ahead = lax.rem(z + n, NZ) * (2 * NY)
            for gx, gb in plane:
                pl.semaphore_signal(barrier, inc=1, device_id=(gx, gb + ahead), device_id_type=MESH)
            return carry

        lax.fori_loop(1, NZ, greet, 0)
        for gx, gb in plane[1:]:
            pl.semaphore_signal(barrier, inc=1, device_id=(gx, gb + z * (2 * NY)), device_id_type=MESH)
        pl.semaphore_signal(barrier, inc=1, device_id=pair, device_id_type=MESH)

    held = emb.shape[0]
    before = (iota((held, held), 0) < iota((held, held), 1)).astype(F32).astype(BF16)
    label_load.wait()
    owner_of = lax.div(labels[...], 2)
    chosen = (iota((64, held), 0) == owner_of).astype(F32)
    count = jnp.dot(chosen.astype(BF16), before, preferred_element_type=F32)
    position = jnp.sum(chosen * count, axis=0, keepdims=True).astype(jnp.int32)
    flat = owner_of * CAP + position
    at_lane = jnp.where(lax.rem(iota((128, held), 0), CAP) == position, 1 + lax.rem(labels[...], 2), 0).astype(F32)
    marks[...] = lax.dot_general(
        chosen.astype(BF16), at_lane.astype(BF16), (((1,), (1,)), ((), ())), preferred_element_type=F32
    )

    for n in range(held // LOAD):
        load(n).wait()
        part = pl.ds(n * LOAD, LOAD)
        values = emb[part, :].astype(F32)
        scale = lax.rsqrt(jnp.sum(values * values, axis=1, keepdims=True) + 1e-06)
        emb[part, :] = (values * scale).astype(BF16)

    def targets(i):
        out = []
        for j in range(8):
            dz = z_offset(lax.rem(i + j, 8))
            dy, h = j // 2, j % 2
            q = lax.rem(parity + dy + dz, 2)
            to = (lax.rem(x + 2 * h + q, NX), lax.rem(y + dy, NY), lax.rem(z + dz, NZ))
            out.append((to[2] * 8 + to[1] * 2 + lax.div(to[0], 2), q, device(*to, c)))
        return out

    def pack(i, to):
        chosen_rows = jnp.concatenate(
            [jnp.where(iota((CAP, held), 0) == flat - b * CAP, 1.0, 0.0) for b, _, _ in to], axis=0
        ).astype(BF16)
        src[pl.ds(pl.multiple_of(i * 128, 128), 128), :] = jnp.dot(
            chosen_rows, emb[...], preferred_element_type=F32
        ).astype(BF16)

    def copies(i, j, b, q):
        slot = 2 * j + q
        return (
            src.at[pl.ds(pl.multiple_of(i * 128 + j * CAP, CAP), CAP)],
            rows.at[i, pl.ds(pl.multiple_of(slot * CAP, CAP), CAP)],
            marks.at[pl.ds(b, 1)],
            row_marks_in.at[i, pl.ds(slot, 1)],
        )

    def send(i, j, b, q, where):
        s, d, ms, md = copies(i, j, b, q)
        remote(s, d, send_sem, recv_sem.at[i], where).start()
        remote(ms, md, mark_send_sem, mark_recv_sem.at[i], where).start()

    first = targets(0)
    pack(0, first)
    pl.semaphore_wait(barrier, 64)
    for j in range(8):
        b, q, where = first[j]
        if j == 0:

            @pl.when(is_owner)
            def _():
                s, d, ms, md = copies(0, 0, b, 0)
                pltpu.make_async_copy(s, d, recv_sem.at[0]).start()
                pltpu.make_async_copy(ms, md, mark_recv_sem.at[0]).start()

            @pl.when(jnp.logical_not(is_owner))
            def _():
                send(0, 0, b, q, where)
        else:
            send(0, j, b, q, where)

    def step(i, carry):
        to = targets(i)
        pack(i, to)
        for j in range(8):
            send(i, j, *to[j])
        return carry

    lax.fori_loop(1, STEPS, step, 0)

    @pl.when(is_owner)
    def _():
        lane = iota((16, 128), 1)
        mine = lax.div(lane, CAP) == lax.rem(iota((16, 128), 0), 8)
        diagonal = lax.rem(iota((16, CAP, 128), 2), 128) == iota((16, CAP, 128), 1)

        def spread(i, half):
            m = row_marks_in[i, pl.ds(half * 16, 16), :]
            column = jnp.sum(jnp.where(diagonal, m.reshape(16, 1, 128), 0.0), axis=2, keepdims=True)
            row_marks[i, pl.ds(half * GROUP, GROUP), :] = jnp.broadcast_to(column, (16, CAP, 128)).reshape(GROUP, 128)
            return m

        def tile(k, first_row, size, col, diag=False):
            left = rows[k, pl.ds(first_row, size), :]
            right = rows[col, pl.ds(0, GROUP), :]
            sim = lax.dot_general(left, right, (((1,), (1,)), ((), ())), preferred_element_type=F32)
            m = row_marks[k, pl.ds(first_row, size), :]
            keep = jnp.concatenate([m, m], axis=1) == col_marks[col, 0:1, :]
            if diag:
                keep = keep & (iota((size, GROUP), 0) != iota((size, GROUP), 1))
            return jnp.max(jnp.where(keep, sim, -1.0).reshape(size // 8, 8, GROUP), axis=0)

        def loop(n, body, init):
            if isinstance(n, int):
                for k in range(n):
                    init = body(k, init)
                return init
            return lax.fori_loop(0, n, body, init)

        def group(i, carry):
            arrived(rows.at[i, pl.ds(0, GROUP)], recv_sem.at[i])
            arrived(row_marks_in.at[i, pl.ds(0, 16)], mark_recv_sem.at[i])
            remote(
                rows.at[i, pl.ds(0, GROUP)], rows.at[i, pl.ds(GROUP, GROUP)], pair_send_sem, pair_recv_sem.at[i], pair
            ).start()
            remote(
                row_marks_in.at[i, pl.ds(0, 16)], row_marks_in.at[i, pl.ds(16, 16)], pair_mark_send_sem,
                pair_mark_recv_sem.at[i], pair,
            ).start()
            m = spread(i, 0)
            lanes = jnp.sum(jnp.where(mine, m, 0.0).reshape(2, 8, 128), axis=1)
            col_marks[i] = jnp.broadcast_to(jnp.concatenate([lanes[0:1], lanes[1:2]], axis=1), (8, GROUP))

            def earlier(k, top):
                best[k] = jnp.maximum(best[k], tile(i, 0, GROUP, k))
                return jnp.maximum(top, tile(k, 0, 2 * GROUP, i))

            top = loop(i, earlier, tile(i, 0, GROUP, i, diag=True))
            arrived(rows.at[i, pl.ds(GROUP, GROUP)], pair_recv_sem.at[i])
            arrived(row_marks_in.at[i, pl.ds(16, 16)], pair_mark_recv_sem.at[i])
            spread(i, 1)
            best[i] = jnp.maximum(top, tile(i, GROUP, GROUP, i))

            def others(k, carry):
                best[k] = jnp.maximum(best[k], tile(i, GROUP, GROUP, k))
                return carry

            loop(i, others, 0)
            return carry

        lax.fori_loop(0, STEPS - UNROLLED, group, 0)
        for i in range(STEPS - UNROLLED, STEPS):
            group(i, 0)
        for i in range(STEPS):
            top = jnp.max(best[i], axis=0, keepdims=True)
            result[pl.ds(2 * i, 1), :] = top[:, 0:128]
            result[pl.ds(2 * i + 1, 1), :] = top[:, 128:256]
        me = z * 8 + y * 2 + lax.div(x, 2)
        line = []
        for n in range(NX * NY):
            dx, dy = n % NX, n // NX
            sx, sy = lax.rem(x - dx + NX, NX), lax.rem(y - dy + NY, NY)
            line.append((dy * 2 + dx // 2, device(sx, sy, 0, c)))

        def give(sz, carry):
            dz = lax.rem(z - sz + NZ, NZ)
            t = jnp.where(dz <= NZ // 2, jnp.maximum(2 * dz - 1, 0), 2 * NZ - 2 * dz)
            for n, (j, (gx, gb)) in enumerate(line):
                i = lax.rem(t - j + 8, 8)
                ours, theirs = result.at[pl.ds(2 * i + j // 4, 1)], results.at[pl.ds(me, 1)]

                def away(ours=ours, theirs=theirs, where=(gx, gb + sz * (2 * NY))):
                    remote(ours, theirs, result_send_sem, result_recv_sem, where).start()

                if n == 0:

                    @pl.when(sz == z)
                    def _():
                        pltpu.make_async_copy(ours, theirs, result_recv_sem).start()

                    pl.when(sz != z)(away)
                else:
                    away()
            return carry

        lax.fori_loop(0, NZ, give, 0)

    arrived(results, result_recv_sem)

    b = iota((64, 128), 0)
    oz, oy = lax.div(b, 8), lax.rem(lax.div(b, 2), NY)
    ox = 2 * lax.rem(b, 2) + lax.rem(oy + oz, 2)
    dx = lax.rem(ox - x + NX, NX)
    j = lax.rem(oy - y + NY, NY) * 2 + lax.div(dx, 2)
    ours = lax.div(iota((64, 128), 1), CAP) == lax.rem(j, 4) * 2 + lax.rem(dx, 2)
    left = jnp.where(ours, results[...], 0.0)
    left = jnp.concatenate([left, jnp.zeros((64, 128), F32)], axis=0).T
    owner_of = lax.div(labels[...], 2)
    chosen = (iota((128, held), 0) == owner_of).astype(F32).astype(BF16)
    spread_out = jnp.zeros((128, held), F32)
    for _ in range(3):
        term = left.astype(BF16)
        spread_out = spread_out + jnp.dot(term, chosen, preferred_element_type=F32)
        left = left - term.astype(F32)
    hit = lax.rem(iota((128, held), 0), CAP) == position
    out[...] = jnp.sum(jnp.where(hit, spread_out, 0.0), axis=0, keepdims=True)

    @pl.when(is_owner)
    def _():
        arrived(src.at[pl.ds(0, 63 * CAP)], send_sem)
        arrived(marks.at[pl.ds(0, 63)], mark_send_sem)
        arrived(rows.at[pl.ds(0, 4)], pair_send_sem)
        arrived(row_marks_in.at[pl.ds(0, 4)], pair_mark_send_sem)

        arrived(row_marks.at[0, pl.ds(0, 127)], result_send_sem)

    @pl.when(jnp.logical_not(is_owner))
    def _():
        arrived(src, send_sem)
        arrived(marks, mark_send_sem)


def shards(embeddings, labels):
    held = embeddings.shape[0]
    dma = pltpu.SemaphoreType.DMA
    best = pl.pallas_call(
        kernel,
        out_shape=jax.ShapeDtypeStruct((1, held), F32),
        in_specs=[pl.BlockSpec(memory_space=pl.ANY)] * 2,
        out_specs=pl.BlockSpec(memory_space=pltpu.VMEM),
        scratch_shapes=[
            pltpu.VMEM((held, D), BF16),
            pltpu.VMEM((1, held), jnp.int32),
            pltpu.VMEM((STEPS * 8 * CAP, D), BF16),
            pltpu.VMEM((64, 128), F32),
            pltpu.VMEM((STEPS, 2 * GROUP, D), BF16),
            pltpu.VMEM((STEPS, 32, 128), F32),
            pltpu.VMEM((STEPS, 2 * GROUP, 128), F32),
            pltpu.VMEM((STEPS, 8, GROUP), F32),
            pltpu.VMEM((STEPS, 8, GROUP), F32),
            pltpu.VMEM((16, 128), F32),
            pltpu.VMEM((64, 128), F32),
            dma((held // LOAD,)), dma, dma, dma((STEPS,)), dma, dma((STEPS,)), dma, dma((STEPS,)), dma, dma((STEPS,)), dma, dma,
        ],
        compiler_params=pltpu.CompilerParams(
            collective_id=0, has_side_effects=True, vmem_limit_bytes=62 * 2**20
        ),
    )(embeddings, labels.reshape(1, held))
    return best.reshape(held)


def solution(mesh):
    in_specs = (P(("grp", "blk"), None), P(("grp", "blk")))
    out_specs = P(("grp", "blk"))
    return jax.shard_map(shards, mesh=mesh, in_specs=in_specs, out_specs=out_specs, check_vma=False)
```

```python
import functools

import jax
import jax.numpy as jnp
from jax import lax
from jax.experimental import pallas as pl
from jax.experimental.pallas import tpu as pltpu
from jax.sharding import PartitionSpec as P

MESH = pl.DeviceIdType.MESH
F32 = jnp.float32
BF16 = jnp.bfloat16

NX, NY, NZ = 4, 4, 8
CAP = 16
STEPS = 8
GROUP = 256
D = 1024
UNROLLED = 2
LOAD = 128


def place():
    x, b = lax.axis_index("grp"), lax.axis_index("blk")
    return x, lax.rem(lax.div(b, 2), NY), lax.div(b, 2 * NY), lax.rem(b, 2)


def device(x, y, z, c):
    return (x, z * (2 * NY) + y * 2 + c)


def z_offset(t):
    return jnp.where(lax.rem(t, 2) == 1, lax.div(t + 1, 2), lax.rem(NZ - lax.div(t, 2), NZ))


def remote(src, dst, send, recv, where):
    return pltpu.make_async_remote_copy(
        src_ref=src, dst_ref=dst, send_sem=send, recv_sem=recv, device_id=where, device_id_type=MESH
    )


def arrived(ref, sem):
    pltpu.make_async_copy(ref, ref, sem).wait()


def iota(shape, dim):
    return lax.broadcasted_iota(jnp.int32, shape, dim)


def kernel(
    emb_hbm, labels_hbm, out, emb, labels, src, marks, rows, row_marks_in, row_marks, col_marks, best, result, results,
    load_sem, label_sem, send_sem, recv_sem, mark_send_sem, mark_recv_sem, pair_send_sem, pair_recv_sem, pair_mark_send_sem,
    pair_mark_recv_sem, result_send_sem, result_recv_sem,
):
    x, y, z, c = place()
    parity = lax.rem(x + y + z, 2)
    is_owner = parity == 0
    pair = device(x, y, z, 1 - c)

    label_load = pltpu.make_async_copy(labels_hbm, labels, label_sem)
    label_load.start()

    def load(n):
        part = pl.ds(n * LOAD, LOAD)
        return pltpu.make_async_copy(emb_hbm.at[part], emb.at[part], load_sem.at[n])

    for n in range(emb.shape[0] // LOAD):
        load(n).start()
    barrier = pltpu.get_barrier_semaphore()

    @pl.when(is_owner)
    def _():
        plane = [device(lax.rem(x + n % NX, NX), lax.rem(y + n // NX, NY), 0, c) for n in range(NX * NY)]

        def greet(n, carry):
            ahead = lax.rem(z + n, NZ) * (2 * NY)
            for gx, gb in plane:
                pl.semaphore_signal(barrier, inc=1, device_id=(gx, gb + ahead), device_id_type=MESH)
            return carry

        lax.fori_loop(1, NZ, greet, 0)
        for gx, gb in plane[1:]:
            pl.semaphore_signal(barrier, inc=1, device_id=(gx, gb + z * (2 * NY)), device_id_type=MESH)
        pl.semaphore_signal(barrier, inc=1, device_id=pair, device_id_type=MESH)

    held = emb.shape[0]
    before = (iota((held, held), 0) < iota((held, held), 1)).astype(F32).astype(BF16)
    label_load.wait()
    owner_of = lax.div(labels[...], 2)
    chosen = (iota((64, held), 0) == owner_of).astype(F32)
    count = jnp.dot(chosen.astype(BF16), before, preferred_element_type=F32)
    position = jnp.sum(chosen * count, axis=0, keepdims=True).astype(jnp.int32)
    flat = owner_of * CAP + position
    at_lane = jnp.where(lax.rem(iota((128, held), 0), CAP) == position, 1 + lax.rem(labels[...], 2), 0).astype(F32)
    marks[...] = lax.dot_general(
        chosen.astype(BF16), at_lane.astype(BF16), (((1,), (1,)), ((), ())), preferred_element_type=F32
    )

    for n in range(held // LOAD):
        load(n).wait()
        part = pl.ds(n * LOAD, LOAD)
        values = emb[part, :].astype(F32)
        scale = lax.rsqrt(jnp.sum(values * values, axis=1, keepdims=True) + 1e-06)
        emb[part, :] = (values * scale).astype(BF16)

    def targets(i):
        out = []
        for j in range(8):
            dz = z_offset(lax.rem(i + j, 8))
            dy, h = j // 2, j % 2
            q = lax.rem(parity + dy + dz, 2)
            to = (lax.rem(x + 2 * h + q, NX), lax.rem(y + dy, NY), lax.rem(z + dz, NZ))
            out.append((to[2] * 8 + to[1] * 2 + lax.div(to[0], 2), q, device(*to, c)))
        return out

    def pack(i, to):
        chosen_rows = jnp.concatenate(
            [jnp.where(iota((CAP, held), 0) == flat - b * CAP, 1.0, 0.0) for b, _, _ in to], axis=0
        ).astype(BF16)
        src[pl.ds(pl.multiple_of(i * 128, 128), 128), :] = jnp.dot(
            chosen_rows, emb[...], preferred_element_type=F32
        ).astype(BF16)

    def copies(i, j, b, q):
        slot = 2 * j + q
        return (
            src.at[pl.ds(pl.multiple_of(i * 128 + j * CAP, CAP), CAP)],
            rows.at[i, pl.ds(pl.multiple_of(slot * CAP, CAP), CAP)],
            marks.at[pl.ds(b, 1)],
            row_marks_in.at[i, pl.ds(slot, 1)],
        )

    def send(i, j, b, q, where):
        s, d, ms, md = copies(i, j, b, q)
        remote(s, d, send_sem, recv_sem.at[i], where).start()
        remote(ms, md, mark_send_sem, mark_recv_sem.at[i], where).start()

    first = targets(0)
    pack(0, first)
    pl.semaphore_wait(barrier, 64)
    for j in range(8):
        b, q, where = first[j]
        if j == 0:

            @pl.when(is_owner)
            def _():
                s, d, ms, md = copies(0, 0, b, 0)
                pltpu.make_async_copy(s, d, recv_sem.at[0]).start()
                pltpu.make_async_copy(ms, md, mark_recv_sem.at[0]).start()

            @pl.when(jnp.logical_not(is_owner))
            def _():
                send(0, 0, b, q, where)
        else:
            send(0, j, b, q, where)

    def step(i, carry):
        to = targets(i)
        pack(i, to)
        for j in range(8):
            send(i, j, *to[j])
        return carry

    lax.fori_loop(1, STEPS, step, 0)

    @pl.when(is_owner)
    def _():
        lane = iota((16, 128), 1)
        mine = lax.div(lane, CAP) == lax.rem(iota((16, 128), 0), 8)
        diagonal = lax.rem(iota((16, CAP, 128), 2), 128) == iota((16, CAP, 128), 1)

        def spread(i, half):
            m = row_marks_in[i, pl.ds(half * 16, 16), :]
            column = jnp.sum(jnp.where(diagonal, m.reshape(16, 1, 128), 0.0), axis=2, keepdims=True)
            row_marks[i, pl.ds(half * GROUP, GROUP), :] = jnp.broadcast_to(column, (16, CAP, 128)).reshape(GROUP, 128)
            return m

        def tile(k, first_row, size, col, diag=False):
            left = rows[k, pl.ds(first_row, size), :]
            right = rows[col, pl.ds(0, GROUP), :]
            sim = lax.dot_general(left, right, (((1,), (1,)), ((), ())), preferred_element_type=F32)
            m = row_marks[k, pl.ds(first_row, size), :]
            keep = jnp.concatenate([m, m], axis=1) == col_marks[col, 0:1, :]
            if diag:
                keep = keep & (iota((size, GROUP), 0) != iota((size, GROUP), 1))
            return jnp.max(jnp.where(keep, sim, -1.0).reshape(size // 8, 8, GROUP), axis=0)

        def loop(n, body, init):
            if isinstance(n, int):
                for k in range(n):
                    init = body(k, init)
                return init
            return lax.fori_loop(0, n, body, init)

        def group(i, carry):
            arrived(rows.at[i, pl.ds(0, GROUP)], recv_sem.at[i])
            arrived(row_marks_in.at[i, pl.ds(0, 16)], mark_recv_sem.at[i])
            remote(
                rows.at[i, pl.ds(0, GROUP)], rows.at[i, pl.ds(GROUP, GROUP)], pair_send_sem, pair_recv_sem.at[i], pair
            ).start()
            remote(
                row_marks_in.at[i, pl.ds(0, 16)], row_marks_in.at[i, pl.ds(16, 16)], pair_mark_send_sem,
                pair_mark_recv_sem.at[i], pair,
            ).start()
            m = spread(i, 0)
            lanes = jnp.sum(jnp.where(mine, m, 0.0).reshape(2, 8, 128), axis=1)
            col_marks[i] = jnp.broadcast_to(jnp.concatenate([lanes[0:1], lanes[1:2]], axis=1), (8, GROUP))

            def earlier(k, top):
                best[k] = jnp.maximum(best[k], tile(i, 0, GROUP, k))
                return jnp.maximum(top, tile(k, 0, 2 * GROUP, i))

            top = loop(i, earlier, tile(i, 0, GROUP, i, diag=True))
            arrived(rows.at[i, pl.ds(GROUP, GROUP)], pair_recv_sem.at[i])
            arrived(row_marks_in.at[i, pl.ds(16, 16)], pair_mark_recv_sem.at[i])
            spread(i, 1)
            best[i] = jnp.maximum(top, tile(i, GROUP, GROUP, i))

            def others(k, carry):
                best[k] = jnp.maximum(best[k], tile(i, GROUP, GROUP, k))
                return carry

            loop(i, others, 0)
            return carry

        lax.fori_loop(0, STEPS - UNROLLED, group, 0)
        for i in range(STEPS - UNROLLED, STEPS):
            group(i, 0)
        for i in range(STEPS):
            top = jnp.max(best[i], axis=0, keepdims=True)
            result[pl.ds(2 * i, 1), :] = top[:, 0:128]
            result[pl.ds(2 * i + 1, 1), :] = top[:, 128:256]
        me = z * 8 + y * 2 + lax.div(x, 2)
        line = []
        for n in range(NX * NY):
            dx, dy = n % NX, n // NX
            sx, sy = lax.rem(x - dx + NX, NX), lax.rem(y - dy + NY, NY)
            line.append((dy * 2 + dx // 2, device(sx, sy, 0, c)))

        def give(sz, carry):
            dz = lax.rem(z - sz + NZ, NZ)
            t = jnp.where(dz <= NZ // 2, jnp.maximum(2 * dz - 1, 0), 2 * NZ - 2 * dz)
            for n, (j, (gx, gb)) in enumerate(line):
                i = lax.rem(t - j + 8, 8)
                ours, theirs = result.at[pl.ds(2 * i + j // 4, 1)], results.at[pl.ds(me, 1)]

                def away(ours=ours, theirs=theirs, where=(gx, gb + sz * (2 * NY))):
                    remote(ours, theirs, result_send_sem, result_recv_sem, where).start()

                if n == 0:

                    @pl.when(sz == z)
                    def _():
                        pltpu.make_async_copy(ours, theirs, result_recv_sem).start()

                    pl.when(sz != z)(away)
                else:
                    away()
            return carry

        lax.fori_loop(0, NZ, give, 0)

    arrived(results, result_recv_sem)

    b = iota((64, 128), 0)
    oz, oy = lax.div(b, 8), lax.rem(lax.div(b, 2), NY)
    ox = 2 * lax.rem(b, 2) + lax.rem(oy + oz, 2)
    dx = lax.rem(ox - x + NX, NX)
    j = lax.rem(oy - y + NY, NY) * 2 + lax.div(dx, 2)
    ours = lax.div(iota((64, 128), 1), CAP) == lax.rem(j, 4) * 2 + lax.rem(dx, 2)
    left = jnp.where(ours, results[...], 0.0)
    left = jnp.concatenate([left, jnp.zeros((64, 128), F32)], axis=0).T
    owner_of = lax.div(labels[...], 2)
    chosen = (iota((128, held), 0) == owner_of).astype(F32).astype(BF16)
    terms = []
    for _ in range(3):
        terms.append(left.astype(BF16))
        left = left - terms[-1].astype(F32)
    found = jnp.dot(jnp.concatenate(terms, axis=0), chosen, preferred_element_type=F32)
    spread_out = found[0:128] + found[128:256] + found[256:384]
    hit = lax.rem(iota((128, held), 0), CAP) == position
    out[...] = jnp.sum(jnp.where(hit, spread_out, 0.0), axis=0, keepdims=True)

    @pl.when(is_owner)
    def _():
        arrived(src.at[pl.ds(0, 63 * CAP)], send_sem)
        arrived(marks.at[pl.ds(0, 63)], mark_send_sem)
        arrived(rows.at[pl.ds(0, 4)], pair_send_sem)
        arrived(row_marks_in.at[pl.ds(0, 4)], pair_mark_send_sem)

        arrived(row_marks.at[0, pl.ds(0, 127)], result_send_sem)

    @pl.when(jnp.logical_not(is_owner))
    def _():
        arrived(src, send_sem)
        arrived(marks, mark_send_sem)


def shards(embeddings, labels):
    held = embeddings.shape[0]
    dma = pltpu.SemaphoreType.DMA
    best = pl.pallas_call(
        kernel,
        out_shape=jax.ShapeDtypeStruct((1, held), F32),
        in_specs=[pl.BlockSpec(memory_space=pl.ANY)] * 2,
        out_specs=pl.BlockSpec(memory_space=pltpu.VMEM),
        scratch_shapes=[
            pltpu.VMEM((held, D), BF16),
            pltpu.VMEM((1, held), jnp.int32),
            pltpu.VMEM((STEPS * 8 * CAP, D), BF16),
            pltpu.VMEM((64, 128), F32),
            pltpu.VMEM((STEPS, 2 * GROUP, D), BF16),
            pltpu.VMEM((STEPS, 32, 128), F32),
            pltpu.VMEM((STEPS, 2 * GROUP, 128), F32),
            pltpu.VMEM((STEPS, 8, GROUP), F32),
            pltpu.VMEM((STEPS, 8, GROUP), F32),
            pltpu.VMEM((16, 128), F32),
            pltpu.VMEM((64, 128), F32),
            dma((held // LOAD,)), dma, dma, dma((STEPS,)), dma, dma((STEPS,)), dma, dma((STEPS,)), dma, dma((STEPS,)), dma, dma,
        ],
        compiler_params=pltpu.CompilerParams(
            collective_id=0, has_side_effects=True, vmem_limit_bytes=55000 * 1024
        ),
    )(embeddings, labels.reshape(1, held))
    return best.reshape(held)


def solution(mesh):
    in_specs = (P(("grp", "blk"), None), P(("grp", "blk")))
    out_specs = P(("grp", "blk"))
    return jax.shard_map(shards, mesh=mesh, in_specs=in_specs, out_specs=out_specs, check_vma=False)
```

```python
import functools

import jax
import jax.numpy as jnp
from jax import lax
from jax.experimental import pallas as pl
from jax.experimental.pallas import tpu as pltpu
from jax.sharding import PartitionSpec as P

MESH = pl.DeviceIdType.MESH
F32 = jnp.float32
BF16 = jnp.bfloat16

NX, NY, NZ = 4, 4, 8
CAP = 16
STEPS = 8
GROUP = 256
D = 1024
UNROLLED = 2
LOAD = 128


def place():
    x, b = lax.axis_index("grp"), lax.axis_index("blk")
    return x, lax.rem(lax.div(b, 2), NY), lax.div(b, 2 * NY), lax.rem(b, 2)


def device(x, y, z, c):
    return (x, z * (2 * NY) + y * 2 + c)


def z_offset(t):
    return jnp.where(lax.rem(t, 2) == 1, lax.div(t + 1, 2), lax.rem(NZ - lax.div(t, 2), NZ))


def remote(src, dst, send, recv, where):
    return pltpu.make_async_remote_copy(
        src_ref=src, dst_ref=dst, send_sem=send, recv_sem=recv, device_id=where, device_id_type=MESH
    )


def arrived(ref, sem):
    pltpu.make_async_copy(ref, ref, sem).wait()


def iota(shape, dim):
    return lax.broadcasted_iota(jnp.int32, shape, dim)


def kernel(
    emb_hbm, labels_hbm, out, emb, labels, src, marks, rows, row_marks_in, row_marks, col_marks, best, result, results,
    load_sem, label_sem, send_sem, recv_sem, mark_send_sem, mark_recv_sem, pair_send_sem, pair_recv_sem, pair_mark_send_sem,
    pair_mark_recv_sem, result_send_sem, result_recv_sem,
):
    x, y, z, c = place()
    parity = lax.rem(x + y + z, 2)
    is_owner = parity == 0
    pair = device(x, y, z, 1 - c)

    label_load = pltpu.make_async_copy(labels_hbm, labels, label_sem)
    label_load.start()

    def load(n):
        part = pl.ds(n * LOAD, LOAD)
        return pltpu.make_async_copy(emb_hbm.at[part], emb.at[part], load_sem.at[n])

    for n in range(emb.shape[0] // LOAD):
        load(n).start()
    barrier = pltpu.get_barrier_semaphore()

    @pl.when(is_owner)
    def _():
        plane = [device(lax.rem(x + n % NX, NX), lax.rem(y + n // NX, NY), 0, c) for n in range(NX * NY)]

        def greet(n, carry):
            ahead = lax.rem(z + n, NZ) * (2 * NY)
            for gx, gb in plane:
                pl.semaphore_signal(barrier, inc=1, device_id=(gx, gb + ahead), device_id_type=MESH)
            return carry

        for gx, gb in plane[1:]:
            pl.semaphore_signal(barrier, inc=1, device_id=(gx, gb + z * (2 * NY)), device_id_type=MESH)
        lax.fori_loop(1, NZ, greet, 0, unroll=True)
        pl.semaphore_signal(barrier, inc=1, device_id=pair, device_id_type=MESH)

    held = emb.shape[0]
    before = (iota((held, held), 0) < iota((held, held), 1)).astype(F32).astype(BF16)
    label_load.wait()
    owner_of = lax.div(labels[...], 2)
    chosen = (iota((64, held), 0) == owner_of).astype(F32)
    count = jnp.dot(chosen.astype(BF16), before, preferred_element_type=F32)
    position = jnp.sum(chosen * count, axis=0, keepdims=True).astype(jnp.int32)
    flat = owner_of * CAP + position
    at_lane = jnp.where(lax.rem(iota((128, held), 0), CAP) == position, 1 + lax.rem(labels[...], 2), 0).astype(F32)
    marks[...] = lax.dot_general(
        chosen.astype(BF16), at_lane.astype(BF16), (((1,), (1,)), ((), ())), preferred_element_type=F32
    )

    for n in range(held // LOAD):
        load(n).wait()
        part = pl.ds(n * LOAD, LOAD)
        values = emb[part, :].astype(F32)
        scale = lax.rsqrt(jnp.sum(values * values, axis=1, keepdims=True) + 1e-06)
        emb[part, :] = (values * scale).astype(BF16)

    def targets(i):
        out = []
        for j in range(8):
            dz = z_offset(lax.rem(i + j, 8))
            dy, h = j // 2, j % 2
            q = lax.rem(parity + dy + dz, 2)
            to = (lax.rem(x + 2 * h + q, NX), lax.rem(y + dy, NY), lax.rem(z + dz, NZ))
            out.append((to[2] * 8 + to[1] * 2 + lax.div(to[0], 2), q, device(*to, c)))
        return out

    def pack(i, to):
        chosen_rows = jnp.concatenate(
            [jnp.where(iota((CAP, held), 0) == flat - b * CAP, 1.0, 0.0) for b, _, _ in to], axis=0
        ).astype(BF16)
        src[pl.ds(pl.multiple_of(i * 128, 128), 128), :] = jnp.dot(
            chosen_rows, emb[...], preferred_element_type=F32
        ).astype(BF16)

    def copies(i, j, b, q):
        slot = 2 * j + q
        return (
            src.at[pl.ds(pl.multiple_of(i * 128 + j * CAP, CAP), CAP)],
            rows.at[i, pl.ds(pl.multiple_of(slot * CAP, CAP), CAP)],
            marks.at[pl.ds(b, 1)],
            row_marks_in.at[i, pl.ds(slot, 1)],
        )

    def send(i, j, b, q, where):
        s, d, ms, md = copies(i, j, b, q)
        remote(s, d, send_sem, recv_sem.at[i], where).start()
        remote(ms, md, mark_send_sem, mark_recv_sem.at[i], where).start()

    first = targets(0)
    pack(0, first)
    pl.semaphore_wait(barrier, 64)
    for j in range(8):
        b, q, where = first[j]
        if j == 0:

            @pl.when(is_owner)
            def _():
                s, d, ms, md = copies(0, 0, b, 0)
                pltpu.make_async_copy(s, d, recv_sem.at[0]).start()
                pltpu.make_async_copy(ms, md, mark_recv_sem.at[0]).start()

            @pl.when(jnp.logical_not(is_owner))
            def _():
                send(0, 0, b, q, where)
        else:
            send(0, j, b, q, where)

    def step(i, carry):
        to = targets(i)
        pack(i, to)
        for j in range(8):
            send(i, j, *to[j])
        return carry

    lax.fori_loop(1, STEPS, step, 0)

    @pl.when(is_owner)
    def _():
        lane = iota((16, 128), 1)
        mine = lax.div(lane, CAP) == lax.rem(iota((16, 128), 0), 8)
        diagonal = lax.rem(iota((16, CAP, 128), 2), 128) == iota((16, CAP, 128), 1)

        def spread(i, half):
            m = row_marks_in[i, pl.ds(half * 16, 16), :]
            column = jnp.sum(jnp.where(diagonal, m.reshape(16, 1, 128), 0.0), axis=2, keepdims=True)
            row_marks[i, pl.ds(half * GROUP, GROUP), :] = jnp.broadcast_to(column, (16, CAP, 128)).reshape(GROUP, 128)
            return m

        def tile(k, first_row, size, col, diag=False):
            left = rows[k, pl.ds(first_row, size), :]
            right = rows[col, pl.ds(0, GROUP), :]
            sim = lax.dot_general(left, right, (((1,), (1,)), ((), ())), preferred_element_type=F32)
            m = row_marks[k, pl.ds(first_row, size), :]
            keep = jnp.concatenate([m, m], axis=1) == col_marks[col, 0:1, :]
            if diag:
                keep = keep & (iota((size, GROUP), 0) != iota((size, GROUP), 1))
            return jnp.max(jnp.where(keep, sim, -1.0).reshape(size // 8, 8, GROUP), axis=0)

        def loop(n, body, init):
            if isinstance(n, int):
                for k in range(n):
                    init = body(k, init)
                return init
            return lax.fori_loop(0, n, body, init)

        def group(i, carry):
            arrived(rows.at[i, pl.ds(0, GROUP)], recv_sem.at[i])
            arrived(row_marks_in.at[i, pl.ds(0, 16)], mark_recv_sem.at[i])
            for n in range(4):
                part, there = pl.ds(n * 64, 64), pl.ds(GROUP + n * 64, 64)
                remote(rows.at[i, part], rows.at[i, there], pair_send_sem, pair_recv_sem.at[i], pair).start()
            remote(
                row_marks_in.at[i, pl.ds(0, 16)], row_marks_in.at[i, pl.ds(16, 16)], pair_mark_send_sem,
                pair_mark_recv_sem.at[i], pair,
            ).start()
            m = spread(i, 0)
            lanes = jnp.sum(jnp.where(mine, m, 0.0).reshape(2, 8, 128), axis=1)
            col_marks[i] = jnp.broadcast_to(jnp.concatenate([lanes[0:1], lanes[1:2]], axis=1), (8, GROUP))

            def earlier(k, top):
                best[k] = jnp.maximum(best[k], tile(i, 0, GROUP, k))
                return jnp.maximum(top, tile(k, 0, 2 * GROUP, i))

            top = loop(i, earlier, tile(i, 0, GROUP, i, diag=True))
            arrived(rows.at[i, pl.ds(GROUP, GROUP)], pair_recv_sem.at[i])
            arrived(row_marks_in.at[i, pl.ds(16, 16)], pair_mark_recv_sem.at[i])
            spread(i, 1)
            best[i] = jnp.maximum(top, tile(i, GROUP, GROUP, i))

            def others(k, carry):
                best[k] = jnp.maximum(best[k], tile(i, GROUP, GROUP, k))
                return carry

            loop(i, others, 0)
            return carry

        lax.fori_loop(0, STEPS - UNROLLED, group, 0)
        for i in range(STEPS - UNROLLED, STEPS):
            group(i, 0)
        for i in range(STEPS):
            top = jnp.max(best[i], axis=0, keepdims=True)
            result[pl.ds(2 * i, 1), :] = top[:, 0:128]
            result[pl.ds(2 * i + 1, 1), :] = top[:, 128:256]
        me = z * 8 + y * 2 + lax.div(x, 2)
        line = []
        for n in range(NX * NY):
            dx, dy = n % NX, n // NX
            sx, sy = lax.rem(x - dx + NX, NX), lax.rem(y - dy + NY, NY)
            line.append((dy * 2 + dx // 2, device(sx, sy, 0, c)))

        def give(sz, carry):
            dz = lax.rem(z - sz + NZ, NZ)
            t = jnp.where(dz <= NZ // 2, jnp.maximum(2 * dz - 1, 0), 2 * NZ - 2 * dz)
            for n, (j, (gx, gb)) in enumerate(line):
                i = lax.rem(t - j + 8, 8)
                ours, theirs = result.at[pl.ds(2 * i + j // 4, 1)], results.at[pl.ds(me, 1)]

                def away(ours=ours, theirs=theirs, where=(gx, gb + sz * (2 * NY))):
                    remote(ours, theirs, result_send_sem, result_recv_sem, where).start()

                if n == 0:

                    @pl.when(sz == z)
                    def _():
                        pltpu.make_async_copy(ours, theirs, result_recv_sem).start()

                    pl.when(sz != z)(away)
                else:
                    away()
            return carry

        lax.fori_loop(0, NZ, give, 0)

    arrived(results, result_recv_sem)

    b = iota((64, 128), 0)
    oz, oy = lax.div(b, 8), lax.rem(lax.div(b, 2), NY)
    ox = 2 * lax.rem(b, 2) + lax.rem(oy + oz, 2)
    dx = lax.rem(ox - x + NX, NX)
    j = lax.rem(oy - y + NY, NY) * 2 + lax.div(dx, 2)
    ours = lax.div(iota((64, 128), 1), CAP) == lax.rem(j, 4) * 2 + lax.rem(dx, 2)
    left = jnp.where(ours, results[...], 0.0)
    left = jnp.concatenate([left, jnp.zeros((64, 128), F32)], axis=0).T
    owner_of = lax.div(labels[...], 2)
    chosen = (iota((128, held), 0) == owner_of).astype(F32).astype(BF16)
    terms = []
    for _ in range(3):
        terms.append(left.astype(BF16))
        left = left - terms[-1].astype(F32)
    found = jnp.dot(jnp.concatenate(terms, axis=0), chosen, preferred_element_type=F32)
    spread_out = found[0:128] + found[128:256] + found[256:384]
    hit = lax.rem(iota((128, held), 0), CAP) == position
    out[...] = jnp.sum(jnp.where(hit, spread_out, 0.0), axis=0, keepdims=True)

    @pl.when(is_owner)
    def _():
        arrived(src.at[pl.ds(0, 63 * CAP)], send_sem)
        arrived(marks.at[pl.ds(0, 63)], mark_send_sem)
        arrived(rows.at[pl.ds(0, 4)], pair_send_sem)
        arrived(row_marks_in.at[pl.ds(0, 4)], pair_mark_send_sem)

        arrived(row_marks.at[0, pl.ds(0, 127)], result_send_sem)

    @pl.when(jnp.logical_not(is_owner))
    def _():
        arrived(src, send_sem)
        arrived(marks, mark_send_sem)


def shards(embeddings, labels):
    held = embeddings.shape[0]
    dma = pltpu.SemaphoreType.DMA
    best = pl.pallas_call(
        kernel,
        out_shape=jax.ShapeDtypeStruct((1, held), F32),
        in_specs=[pl.BlockSpec(memory_space=pl.ANY)] * 2,
        out_specs=pl.BlockSpec(memory_space=pltpu.VMEM),
        scratch_shapes=[
            pltpu.VMEM((held, D), BF16),
            pltpu.VMEM((1, held), jnp.int32),
            pltpu.VMEM((STEPS * 8 * CAP, D), BF16),
            pltpu.VMEM((64, 128), F32),
            pltpu.VMEM((STEPS, 2 * GROUP, D), BF16),
            pltpu.VMEM((STEPS, 32, 128), F32),
            pltpu.VMEM((STEPS, 2 * GROUP, 128), F32),
            pltpu.VMEM((STEPS, 8, GROUP), F32),
            pltpu.VMEM((STEPS, 8, GROUP), F32),
            pltpu.VMEM((16, 128), F32),
            pltpu.VMEM((64, 128), F32),
            dma((held // LOAD,)), dma, dma, dma((STEPS,)), dma, dma((STEPS,)), dma, dma((STEPS,)), dma, dma((STEPS,)), dma, dma,
        ],
        compiler_params=pltpu.CompilerParams(
            collective_id=0, has_side_effects=True, vmem_limit_bytes=55000 * 1024
        ),
    )(embeddings, labels.reshape(1, held))
    return best.reshape(held)


def solution(mesh):
    in_specs = (P(("grp", "blk"), None), P(("grp", "blk")))
    out_specs = P(("grp", "blk"))
    return jax.shard_map(shards, mesh=mesh, in_specs=in_specs, out_specs=out_specs, check_vma=False)
```
